32 devices in a mesh: ffn: 8 (over z, core), mp: 4 (over y, x).
Axes of the slice: x: 2, y: 2, z: 4, core: 2. Of those that a mesh axis runs over, the one named last changes fastest.
Arguments:
- hidden_in: bfloat16 [256, 8192], P(None, 'mp'), may hold values from -40 to 40
- norm_gain: float32 [8192], P('mp'), may hold values from 0.1 to 1.9
- grad_out: bfloat16 [256, 8192], P(None, 'mp'), may hold values from -6 to 6
- gate_weight: bfloat16 [8192, 28672], P('mp', 'ffn'), may hold values from -0.0625 to 0.0625
- up_weight: bfloat16 [8192, 28672], P('mp', 'ffn'), may hold values from -0.0625 to 0.0625
- down_weight: bfloat16 [28672, 8192], P('ffn', 'mp'), may hold values from -0.03125 to 0.03125
Outputs:
- grad_hidden: bfloat16 [256, 8192], P(None, 'mp')
- grad_gain: float32 [8192], P('mp')
- grad_gate: bfloat16 [8192, 28672], P('mp', 'ffn')
- grad_up: bfloat16 [8192, 28672], P('mp', 'ffn')
- grad_down: bfloat16 [28672, 8192], P('ffn', 'mp')
The draws below stay inside these ranges and needn't reach their ends.
All inputs are finite; a program needn't handle non-finite values.
Results may differ from the reference program's by a relative error of at most 0.0066.
Values may be sent and summed in bfloat16 or wider, within the bound.
A program may use at most 192 MiB of HBM per device.

```python
import math
import jax
import jax.numpy as jnp
from jax import lax

D = 8192
FF = 28672
TOKENS = 256


def draw_hidden_in(key, part):
    keys = jax.random.split(jax.random.fold_in(key, 17), 3)
    row_scale = jnp.exp(jax.random.uniform(keys[0], (TOKENS, 1), jnp.float32) * math.log(10.0))
    ramp = jnp.linspace(0.0, math.log(3.0), D, dtype=jnp.float32)
    col_scale = jnp.exp(jax.random.uniform(keys[1], (1, D), jnp.float32) * 0.5 * math.log(10.0) + ramp[None, :])
    base = jax.random.normal(keys[2], (TOKENS, D), jnp.float32)
    base = jnp.clip(base, -4.0, 4.0)
    return (base * row_scale * col_scale / 10.0).astype(jnp.bfloat16)


def levels(key, shape, shards, low, high):
    def one(dim, parts):
        heights = jax.random.uniform(jax.random.fold_in(jax.random.fold_in(key, 6), dim), (parts,), jnp.float32, low / len(shards), high / len(shards))
        return jnp.repeat(jnp.exp(heights), shape[dim] // parts).reshape((-1,) + (1,) * (len(shape) - dim - 1))

    gain = one(*shards[0])
    for cut in shards[1:]:
        gain = gain * one(*cut)
    return gain


def scatter_about(key, extent, width, most, shards=(), kind=jnp.bfloat16):
    result = jax.random.normal(key, extent, jnp.float32) * width
    if len(shards) > 0:
        result = levels(key, extent, shards, -0.22, 0.18) * result
    return jnp.clip(result, min=-most, max=most).astype(kind)


def setup_inputs(seed: int = 0) -> dict:
    streams_of = jax.random.split(jax.random.key(seed), 7)
    return {
        "hidden_in": draw_hidden_in(jax.random.fold_in(streams_of[6], 71), 0),
        "norm_gain": jnp.clip(1.0 + 0.18 * jax.random.normal(streams_of[1], (D,), jnp.float32), 0.1, 1.9),
        "grad_out": scatter_about(streams_of[2], (TOKENS, D), 1.0, 6.0, ((1, 4),)),
        "gate_weight": scatter_about(streams_of[3], (D, FF), D ** -0.5, 0.0625, ((0, 4), (1, 8))),
        "up_weight": scatter_about(streams_of[4], (D, FF), D ** -0.5, 0.0625, ((0, 4), (1, 8))),
        "down_weight": scatter_about(streams_of[5], (FF, D), FF ** -0.5, 0.03125, ((0, 8), (1, 4))),
    }


epsilon = 1e-05

def reference(hidden_in, norm_gain, grad_out, gate_weight, up_weight, down_weight):
    hidden = hidden_in.astype(jnp.float32)
    inverse = lax.rsqrt(lax.optimization_barrier(jnp.sum(hidden * hidden, axis=1)) / D + epsilon)
    scaled = (hidden * norm_gain).astype(jnp.bfloat16)
    gate = inverse[:, None] * jnp.dot(scaled, gate_weight, preferred_element_type=jnp.float32)
    up_val = inverse[:, None] * jnp.dot(scaled, up_weight, preferred_element_type=jnp.float32)
    sigma = jax.nn.sigmoid(gate)
    activation = (gate * sigma * up_val).astype(jnp.bfloat16)
    act_grad = jnp.dot(grad_out, down_weight.T, preferred_element_type=jnp.float32)
    grad_down = jnp.dot(activation.T, grad_out, preferred_element_type=jnp.float32).astype(jnp.bfloat16)
    gate_grad = (inverse[:, None] * act_grad * up_val * sigma * (1.0 + gate * (1.0 - sigma))).astype(jnp.bfloat16)
    up_grad = (inverse[:, None] * act_grad * gate * sigma).astype(jnp.bfloat16)
    grad_gate = jnp.dot(scaled.T, gate_grad, preferred_element_type=jnp.float32).astype(jnp.bfloat16)
    grad_up = jnp.dot(scaled.T, up_grad, preferred_element_type=jnp.float32).astype(jnp.bfloat16)
    input_grad = jnp.dot(gate_grad, gate_weight.T, preferred_element_type=jnp.float32) + jnp.dot(up_grad, up_weight.T, preferred_element_type=jnp.float32)
    products = lax.optimization_barrier(jnp.sum(norm_gain * hidden * input_grad, axis=1))
    grad_hidden = (norm_gain * input_grad - hidden * (inverse * inverse * products / D)[:, None]).astype(jnp.bfloat16)
    grad_gain = lax.optimization_barrier(jnp.sum(hidden * input_grad, axis=0))
    return (grad_hidden, grad_gain, grad_gate, grad_up, grad_down)
```

```python
import jax
import jax.numpy as jnp
from jax import lax
from jax.sharding import PartitionSpec as P

epsilon = 1e-05
F32 = jnp.float32
BF16 = jnp.bfloat16


def swap(x, axis, count, bit):
    return lax.ppermute(x, axis, [(i, i ^ bit) for i in range(count)])


def bits_of(count):
    return [1 << b for b in range(count.bit_length() - 1)]


def relative(x, me, count):
    rows = x.shape[0] // count
    parts = [lax.dynamic_slice_in_dim(x, (me ^ r) * rows, rows, 0) for r in range(count)]
    return jnp.concatenate(parts, axis=0)


def all_sum(x, axis, count):
    for bit in bits_of(count):
        x = x + swap(x, axis, count, bit)
    return x


def scatter_sum(x, axis, count, order, types):
    held = list(range(count))
    rows = x.shape[-2] // count
    for bit, kind in zip(order, types):
        keep = [k for k, r in enumerate(held) if not r & bit]
        send = [k for k, r in enumerate(held) if r & bit]
        blocks = [x[..., k * rows:(k + 1) * rows, :] for k in range(len(held))]
        out = jnp.concatenate([blocks[k].astype(kind) for k in send], axis=-2)
        mine = jnp.concatenate([blocks[k] for k in keep], axis=-2)
        x = mine + swap(out, axis, count, bit).astype(F32)
        held = [held[k] for k in keep]
    return x


def gather(x, axis, count, order):
    blocks = {0: x}
    for bit in order:
        have = sorted(blocks)
        rows = x.shape[-2]
        got = swap(jnp.concatenate([blocks[r] for r in have], axis=-2), axis, count, bit)
        for k, r in enumerate(have):
            blocks[r ^ bit] = got[..., k * rows:(k + 1) * rows, :]
    return jnp.concatenate([blocks[r] for r in range(count)], axis=-2)


def dot(a, b, da, db):
    return lax.dot_general(a, b, (((da,), (db,)), ((), ())), preferred_element_type=F32)


def cuts(width):
    if width % 256 == 0 and width >= 1024:
        units = width // 256
        pairs = 2
        sizes = []
        for p in range(pairs * 2):
            sizes.append((units // (2 * pairs) + (1 if p < units % (2 * pairs) else 0)) * 256)
        return sizes
    return [width - width // 2, width // 2]


def build(mp, ffn):
    def body(hidden_in, norm_gain, grad_out, gate_weight, up_weight, down_weight):
        tokens, local = hidden_in.shape
        features = local * mp
        width = gate_weight.shape[1]
        m = lax.axis_index("mp")
        f = lax.axis_index("ffn")
        hidden_r = relative(hidden_in, m, mp)
        grad_out_r = relative(grad_out, m, mp)
        hidden = hidden_in.astype(F32)
        square_sum = all_sum(jnp.sum(hidden * hidden, axis=1), "mp", mp)
        inverse = lax.rsqrt(square_sum / features + epsilon)
        mp_rows = tokens // mp
        mine_inverse = lax.dynamic_slice_in_dim(inverse, m * mp_rows, mp_rows, 0)[:, None]
        scaled = (hidden_r.astype(F32) * norm_gain).astype(BF16)

        order = bits_of(mp)
        input_part = jnp.zeros((tokens, local), F32)
        finals = []
        first = 0
        for piece, size in enumerate(cuts(width)):
            way = order if piece % 2 == 0 else order[::-1]
            cols = slice(first, first + size)
            first += size
            parts = jnp.stack([
                dot(scaled, gate_weight[:, cols], 1, 0),
                dot(scaled, up_weight[:, cols], 1, 0),
                dot(grad_out_r, down_weight[cols, :], 1, 1),
            ])
            sums = scatter_sum(parts, "mp", mp, way, [BF16] * len(way))
            gate = mine_inverse * sums[0]
            up_val = mine_inverse * sums[1]
            act_grad = sums[2]
            sigma = jax.nn.sigmoid(gate)
            activation = (gate * sigma * up_val).astype(BF16)
            gate_grad = (
                mine_inverse * act_grad * up_val * sigma * (1.0 + gate * (1.0 - sigma))
            ).astype(BF16)
            up_grad = (mine_inverse * act_grad * gate * sigma).astype(BF16)
            full = gather(jnp.stack([activation, gate_grad, up_grad]), "mp", mp, way[::-1])
            finals.append(full)
            input_part = input_part + dot(full[1], gate_weight[:, cols], 1, 1)
            input_part = input_part + dot(full[2], up_weight[:, cols], 1, 1)

        activation, gate_grad, up_grad = (
            jnp.concatenate([full[k] for full in finals], axis=1) for k in range(3)
        )
        absolute = relative(input_part, m, mp)
        ffn_order = bits_of(ffn)
        input_grad = scatter_sum(
            relative(absolute, f, ffn), "ffn", ffn, ffn_order, [F32] + [BF16] * (len(ffn_order) - 1)
        )
        grad_gate = dot(scaled, gate_grad, 0, 0).astype(BF16)
        grad_up = dot(scaled, up_grad, 0, 0).astype(BF16)
        grad_down = dot(activation, grad_out_r, 0, 0).astype(BF16)
        row_count = tokens // ffn
        rows_hidden = lax.dynamic_slice_in_dim(hidden, f * row_count, row_count, 0)
        rows_inverse = lax.dynamic_slice_in_dim(inverse, f * row_count, row_count, 0)
        products = all_sum(jnp.sum(norm_gain * rows_hidden * input_grad, axis=1), "mp", mp)
        rows_out = (
            norm_gain * input_grad
            - rows_hidden * (rows_inverse * rows_inverse * products / features)[:, None]
        ).astype(BF16)
        grad_gain = all_sum(jnp.sum(rows_hidden * input_grad, axis=0), "ffn", ffn)
        grad_hidden = relative(gather(rows_out, "ffn", ffn, ffn_order[::-1]), f, ffn)
        return (grad_hidden, grad_gain, grad_gate, grad_up, grad_down)

    return body


def solution(mesh):
    placed = (P(None, "mp"), P("mp"), P(None, "mp"), P("mp", "ffn"), P("mp", "ffn"), P("ffn", "mp"))
    return jax.shard_map(
        build(mesh.shape["mp"], mesh.shape["ffn"]),
        mesh=mesh,
        in_specs=placed,
        out_specs=(P(None, "mp"), P("mp"), P("mp", "ffn"), P("mp", "ffn"), P("ffn", "mp")),
        check_vma=False,
    )
```

```python
import functools

import jax
import jax.numpy as jnp
from jax import lax
from jax.experimental import pallas as pl
from jax.experimental.pallas import tpu as pltpu
from jax.sharding import PartitionSpec as P

epsilon = 1e-05
F32 = jnp.float32
BF16 = jnp.bfloat16


def swap(x, axis, count, bit):
    return lax.ppermute(x, axis, [(i, i ^ bit) for i in range(count)])


def bits_of(count):
    return [1 << b for b in range(count.bit_length() - 1)]


def relative(x, me, count):
    rows = x.shape[0] // count
    parts = [lax.dynamic_slice_in_dim(x, (me ^ r) * rows, rows, 0) for r in range(count)]
    return jnp.concatenate(parts, axis=0)


def all_sum(x, axis, count):
    for bit in bits_of(count):
        x = x + swap(x, axis, count, bit)
    return x


def pick(x, held, wanted, total):
    rows = total // len(held)
    parts = [x[..., k * rows:(k + 1) * rows, :] for k, r in enumerate(held) if r in wanted]
    return jnp.concatenate(parts, axis=-2)


def scatter_sum(mine, out, axis, count, order, types):
    received = swap(out, axis, count, order[0])
    held = [r for r in range(count) if not r & order[0]]
    return finish_sum(mine, received, held, axis, count, order, types)


def finish_sum(x, received, held, axis, count, order, types):
    for bit, kind in zip(order[1:], types[1:]):
        x = x + received.astype(F32)
        keep = [r for r in held if not r & bit]
        send = [r for r in held if r & bit]
        total = x.shape[-2]
        out = pick(x, held, send, total).astype(kind)
        x = pick(x, held, keep, total)
        received = swap(out, axis, count, bit)
        held = keep
    return x, received


def gather(x, axis, count, order):
    blocks = {0: x}
    for bit in order:
        have = sorted(blocks)
        rows = x.shape[-2]
        got = swap(jnp.concatenate([blocks[r] for r in have], axis=-2), axis, count, bit)
        for k, r in enumerate(have):
            blocks[r ^ bit] = got[..., k * rows:(k + 1) * rows, :]
    return jnp.concatenate([blocks[r] for r in range(count)], axis=-2)


def dot(a, b, da, db):
    return lax.dot_general(a, b, (((da,), (db,)), ((), ())), preferred_element_type=F32)


TILE = 256
LIGHT = pl.CostEstimate(flops=1, bytes_accessed=1, transcendentals=0)


def cuts(width):
    if width % TILE == 0 and width // TILE >= 4:
        units = width // TILE
        return [(units // 4 + (1 if p < units % 4 else 0)) * TILE for p in range(4)]
    return [width - width // 2, width // 2]


def forward_kernel(count, bit, scaled, grad_out, gate, up, down, *rest):
    keep, send = rest[-2:]
    rows = scaled.shape[0] // count
    for k in range(3):
        if k < 2:
            part = dot(scaled[...], (gate, up)[k][...], 1, 0)
        else:
            part = dot(grad_out[...], down[...], 1, 1)
        kept = sent = 0
        for r in range(count):
            block = part[r * rows:(r + 1) * rows]
            if r & bit:
                send[k, sent * rows:(sent + 1) * rows, :] = block.astype(BF16)
                sent += 1
            else:
                keep[k, kept * rows:(kept + 1) * rows, :] = block
                kept += 1


def forward(scaled, grad_out, gate_weight, up_weight, down_weight, first, size, count, bit, after):
    tokens, local = scaled.shape
    base = first // TILE
    whole = pl.BlockSpec((tokens, local), lambda j: (0, 0))
    column = pl.BlockSpec((local, TILE), lambda j: (0, base + j))
    result = pl.BlockSpec((3, tokens // 2, TILE), lambda j: (0, 0, j))
    extra = list(after)
    return pl.pallas_call(
        functools.partial(forward_kernel, count, bit),
        grid=(size // TILE,),
        in_specs=[whole, whole, column, column, pl.BlockSpec((TILE, local), lambda j: (base + j, 0))]
        + [pl.BlockSpec(memory_space=pl.ANY)] * len(extra),
        out_specs=[result, result],
        out_shape=[
            jax.ShapeDtypeStruct((3, tokens // 2, size), F32),
            jax.ShapeDtypeStruct((3, tokens // 2, size), BF16),
        ],
        compiler_params=pltpu.CompilerParams(vmem_limit_bytes=32 * 2**20),
        cost_estimate=LIGHT,
    )(scaled, grad_out, gate_weight, up_weight, down_weight, *extra)


def activation_kernel(mine, received, inverse, *rest):
    out = rest[-1]
    scale = inverse[...]
    gate = scale * (mine[0] + received[0].astype(F32))
    up_val = scale * (mine[1] + received[1].astype(F32))
    act_grad = mine[2] + received[2].astype(F32)
    sigma = 1.0 / (1.0 + jnp.exp(-gate))
    out[0] = (gate * sigma * up_val).astype(BF16)
    out[1] = (scale * act_grad * up_val * sigma * (1.0 + gate * (1.0 - sigma))).astype(BF16)
    out[2] = (scale * act_grad * gate * sigma).astype(BF16)


def activate(mine, received, inverse, after):
    _, rows, size = mine.shape
    block = pl.BlockSpec((3, rows, TILE), lambda j: (0, 0, j))
    extra = [] if after is None else [after]
    return pl.pallas_call(
        activation_kernel,
        grid=(size // TILE,),
        in_specs=[block, block, pl.BlockSpec((rows, 1), lambda j: (0, 0))]
        + [pl.BlockSpec(memory_space=pl.ANY)] * len(extra),
        out_specs=block,
        out_shape=jax.ShapeDtypeStruct(mine.shape, BF16),
        cost_estimate=LIGHT,
    )(mine, received, inverse, *extra)


def transpose_kernel(x, after, out):
    out[...] = x[...].T


def transpose(x, after):
    rows, columns = x.shape
    return pl.pallas_call(
        transpose_kernel,
        grid=(columns // TILE,),
        in_specs=[pl.BlockSpec((rows, TILE), lambda j: (0, j)), pl.BlockSpec(memory_space=pl.ANY)],
        out_specs=pl.BlockSpec((TILE, rows), lambda j: (j, 0)),
        out_shape=jax.ShapeDtypeStruct((columns, rows), x.dtype),
        cost_estimate=LIGHT,
    )(x, after)


def rows_kernel(mine, received, hidden, gain, after, total, products, gain_part):
    value = mine[...] + received[...].astype(F32)
    term = hidden[...].astype(F32) * value
    total[...] = value
    products[...] = jnp.sum(term * gain[...], axis=1, keepdims=True)
    gain_part[...] = jnp.sum(term, axis=0, keepdims=True)


def finish_rows(mine, received, hidden, gain, after):
    rows, columns = mine.shape
    vmem = pl.BlockSpec(memory_space=pltpu.VMEM)
    return pl.pallas_call(
        rows_kernel,
        in_specs=[vmem] * 4 + [pl.BlockSpec(memory_space=pl.ANY)],
        out_specs=[vmem] * 3,
        out_shape=[
            jax.ShapeDtypeStruct((rows, columns), F32),
            jax.ShapeDtypeStruct((rows, 1), F32),
            jax.ShapeDtypeStruct((1, columns), F32),
        ],
        cost_estimate=LIGHT,
    )(mine, received, hidden, gain[None, :], after)


def input_step(full, gate, up, before, total):
    @pl.when(pl.program_id(0) == 0)
    def _():
        total[...] = jnp.zeros_like(total) if before is None else before[...]

    total[...] += dot(full[1], gate[...], 1, 1) + dot(full[2], up[...], 1, 1)


def weight_step(full, scaled_t, grad_out, grad_gate, grad_up, grad_down):
    grad_gate[...] = dot(scaled_t[...], full[1], 1, 0).astype(BF16)
    grad_up[...] = dot(scaled_t[...], full[2], 1, 0).astype(BF16)
    grad_down[...] = dot(full[0], grad_out[...], 0, 0).astype(BF16)


def backward_kernel(with_input, with_weights, has_before, has_grads, *refs):
    refs = list(refs)
    full = refs.pop(0)
    if with_input:
        gate, up = refs.pop(0), refs.pop(0)
        before = refs.pop(0) if has_before else None
    if with_weights:
        scaled_t, grad_out = refs.pop(0), refs.pop(0)
        if has_grads:
            refs = refs[3:]
    if with_input:
        input_step(full, gate, up, before, refs.pop(0))
    if with_weights:
        weight_step(full, scaled_t, grad_out, *refs)


def backward(full, first, weights=None, before=None, tall=None, grads=None, shapes=None):
    size = full.shape[2]
    tokens = full.shape[1]
    base = first // TILE
    local = weights[0].shape[0] if weights is not None else tall[0].shape[0]
    column = pl.BlockSpec((local, TILE), lambda j: (0, base + j))
    row = pl.BlockSpec((TILE, local), lambda j: (base + j, 0))
    whole = pl.BlockSpec((tokens, local), lambda j: (0, 0))
    operands = [full]
    in_specs = [pl.BlockSpec((3, tokens, TILE), lambda j: (0, 0, j))]
    out_specs, out_shape, aliases = [], [], {}
    flops = moved = 0
    if weights is not None:
        operands += list(weights)
        in_specs += [column, column]
        if before is not None:
            operands.append(before)
            in_specs.append(whole)
        out_specs.append(whole)
        out_shape.append(jax.ShapeDtypeStruct((tokens, local), F32))
        flops += 4 * tokens * local * size
        moved += 4 * local * size
    if tall is not None:
        operands += list(tall)
        in_specs += [pl.BlockSpec((local, tokens), lambda j: (0, 0)), whole]
        if grads is not None:
            for k in range(3):
                aliases[len(operands) + k] = len(out_shape) + k
            operands += list(grads)
            in_specs += [pl.BlockSpec(memory_space=pl.ANY)] * 3
        out_specs += [column, column, row]
        out_shape += shapes
        flops += 6 * tokens * local * size
        moved += 6 * local * size
    return pl.pallas_call(
        functools.partial(
            backward_kernel, weights is not None, tall is not None, before is not None, grads is not None
        ),
        grid=(size // TILE,),
        in_specs=in_specs,
        out_specs=out_specs,
        out_shape=out_shape,
        input_output_aliases=aliases,
        compiler_params=pltpu.CompilerParams(vmem_limit_bytes=44 * 2**20),
        cost_estimate=LIGHT if weights is not None else pl.CostEstimate(
            flops=flops, bytes_accessed=moved, transcendentals=0
        ),
    )(*operands)


def build(mp, ffn):
    def body(hidden_in, norm_gain, grad_out, gate_weight, up_weight, down_weight):
        tokens, local = hidden_in.shape
        features = local * mp
        width = gate_weight.shape[1]
        m = lax.axis_index("mp")
        f = lax.axis_index("ffn")
        sizes = cuts(width)
        tiled = all(size % TILE == 0 for size in sizes)
        hidden_r = relative(hidden_in, m, mp)
        grad_out_r = relative(grad_out, m, mp)
        scaled = (hidden_r.astype(F32) * norm_gain).astype(BF16)

        order = bits_of(mp)
        blocks = list(range(mp))
        first = 0
        starts, kept, sent, arrived = [], [], [], []
        for piece, size in enumerate(sizes):
            way = order if piece % 2 == 0 else order[::-1]
            cols = slice(first, first + size)
            starts.append(first)
            if tiled:
                keep, send = forward(
                    scaled, grad_out_r, gate_weight, up_weight, down_weight, first, size, mp, way[0],
                    sent[-1:] + arrived[:-1][-1:],
                )
            else:
                parts = jnp.stack([
                    dot(scaled, gate_weight[:, cols], 1, 0),
                    dot(scaled, up_weight[:, cols], 1, 0),
                    dot(grad_out_r, down_weight[cols, :], 1, 1),
                ])
                keep = pick(parts, blocks, [r for r in blocks if not r & way[0]], tokens)
                send = pick(parts, blocks, [r for r in blocks if r & way[0]], tokens).astype(BF16)
            kept.append(keep)
            sent.append(send)
            arrived.append(swap(send, "mp", mp, way[0]))
            first += size

        late, _ = lax.optimization_barrier((hidden_in, sent[0]))
        hidden = late.astype(F32)
        square_sum = all_sum(jnp.sum(hidden * hidden, axis=1), "mp", mp)
        inverse = lax.rsqrt(square_sum / features + epsilon)
        mp_rows = tokens // mp
        mine_inverse = lax.dynamic_slice_in_dim(inverse, m * mp_rows, mp_rows, 0)[:, None]

        shapes = [
            jax.ShapeDtypeStruct(w.shape, BF16) for w in (gate_weight, up_weight, down_weight)
        ]
        scaled_t = transpose(scaled, sent[1]) if tiled else None
        input_part = grads = None
        finals, totals = [], []
        for piece, size in enumerate(sizes):
            way = order if piece % 2 == 0 else order[::-1]
            mine, received = finish_sum(
                kept[piece], arrived[piece], [r for r in blocks if not r & way[0]],
                "mp", mp, way, [BF16] * len(way),
            )
            if tiled:
                results = activate(mine, received, mine_inverse, totals[piece - 2] if piece >= 2 else None)
            else:
                sums = mine + received.astype(F32)
                gate = mine_inverse * sums[0]
                up_val = mine_inverse * sums[1]
                act_grad = sums[2]
                sigma = jax.nn.sigmoid(gate)
                activation = (gate * sigma * up_val).astype(BF16)
                gate_grad = (
                    mine_inverse * act_grad * up_val * sigma * (1.0 + gate * (1.0 - sigma))
                ).astype(BF16)
                up_grad = (mine_inverse * act_grad * gate * sigma).astype(BF16)
                results = jnp.stack([activation, gate_grad, up_grad])
            full = gather(results, "mp", mp, way[::-1])
            finals.append(full)
            begin = starts[piece]
            cols = slice(begin, begin + size)
            if not tiled:
                term = dot(full[1], gate_weight[:, cols], 1, 1) + dot(full[2], up_weight[:, cols], 1, 1)
                input_part = term if input_part is None else input_part + term
            elif piece + 1 < len(sizes):
                input_part, *grads = backward(
                    full, begin, (gate_weight, up_weight), input_part, (scaled_t, grad_out_r), grads, shapes
                )
                totals.append(grads[0])
            else:
                input_part, = backward(full, begin, (gate_weight, up_weight), input_part)
                grads = backward(
                    full, begin, tall=(scaled_t, grad_out_r), grads=grads, shapes=shapes
                )

        if not tiled:
            activation, gate_grad, up_grad = (
                jnp.concatenate([full[k] for full in finals], axis=1) for k in range(3)
            )
            grads = [
                dot(scaled, gate_grad, 0, 0).astype(BF16),
                dot(scaled, up_grad, 0, 0).astype(BF16),
                dot(activation, grad_out_r, 0, 0).astype(BF16),
            ]
        grad_gate, grad_up, grad_down = grads
        ffn_order = bits_of(ffn)
        ordered = relative(relative(input_part, m, mp), f, ffn)
        places = list(range(ffn))
        kinds = [F32] + [BF16] * (len(ffn_order) - 1)
        mine = pick(ordered, places, [r for r in places if not r & ffn_order[0]], tokens)
        away = pick(ordered, places, [r for r in places if r & ffn_order[0]], tokens)
        mine, received = scatter_sum(mine, away.astype(kinds[0]), "ffn", ffn, ffn_order, kinds)
        row_count = tokens // ffn
        rows_in = lax.dynamic_slice_in_dim(hidden_in, f * row_count, row_count, 0)
        rows_hidden = rows_in.astype(F32)
        if tiled:
            input_grad, product_part, gain_part = finish_rows(mine, received, rows_in, norm_gain, grads[0])
            product_part, gain_part = product_part[:, 0], gain_part[0]
        else:
            input_grad = mine + received.astype(F32)
            product_part = jnp.sum(norm_gain * rows_hidden * input_grad, axis=1)
            gain_part = jnp.sum(rows_hidden * input_grad, axis=0)
        rows_inverse = lax.dynamic_slice_in_dim(inverse, f * row_count, row_count, 0)
        products = all_sum(product_part, "mp", mp)
        rows_out = (
            norm_gain * input_grad
            - rows_hidden * (rows_inverse * rows_inverse * products / features)[:, None]
        ).astype(BF16)
        grad_gain = all_sum(gain_part, "ffn", ffn)
        grad_hidden = relative(gather(rows_out, "ffn", ffn, ffn_order[::-1]), f, ffn)
        return (grad_hidden, grad_gain, grad_gate, grad_up, grad_down)

    return body


def solution(mesh):
    placed = (P(None, "mp"), P("mp"), P(None, "mp"), P("mp", "ffn"), P("mp", "ffn"), P("ffn", "mp"))
    return jax.shard_map(
        build(mesh.shape["mp"], mesh.shape["ffn"]),
        mesh=mesh,
        in_specs=placed,
        out_specs=(P(None, "mp"), P("mp"), P("mp", "ffn"), P("mp", "ffn"), P("ffn", "mp")),
        check_vma=False,
    )
```

```python
import functools

import jax
import jax.numpy as jnp
from jax import lax
from jax.experimental import pallas as pl
from jax.experimental.pallas import tpu as pltpu
from jax.sharding import PartitionSpec as P

epsilon = 1e-05
F32 = jnp.float32
BF16 = jnp.bfloat16


def swap(x, axis, count, bit):
    return lax.ppermute(x, axis, [(i, i ^ bit) for i in range(count)])


def bits_of(count):
    return [1 << b for b in range(count.bit_length() - 1)]


def relative(x, me, count):
    rows = x.shape[0] // count
    parts = [lax.dynamic_slice_in_dim(x, (me ^ r) * rows, rows, 0) for r in range(count)]
    return jnp.concatenate(parts, axis=0)


def all_sum(x, axis, count):
    for bit in bits_of(count):
        x = x + swap(x, axis, count, bit)
    return x


def pick(x, held, wanted, total):
    rows = total // len(held)
    parts = [x[..., k * rows:(k + 1) * rows, :] for k, r in enumerate(held) if r in wanted]
    return jnp.concatenate(parts, axis=-2)


def scatter_sum(mine, out, axis, count, order, types):
    received = swap(out, axis, count, order[0])
    held = [r for r in range(count) if not r & order[0]]
    return finish_sum(mine, received, held, axis, count, order, types)


def finish_sum(x, received, held, axis, count, order, types):
    for bit, kind in zip(order[1:], types[1:]):
        x = x + received.astype(F32)
        keep = [r for r in held if not r & bit]
        send = [r for r in held if r & bit]
        total = x.shape[-2]
        out = pick(x, held, send, total).astype(kind)
        x = pick(x, held, keep, total)
        received = swap(out, axis, count, bit)
        held = keep
    return x, received


def gather(x, axis, count, order):
    blocks = {0: x}
    for bit in order:
        have = sorted(blocks)
        rows = x.shape[-2]
        got = swap(jnp.concatenate([blocks[r] for r in have], axis=-2), axis, count, bit)
        for k, r in enumerate(have):
            blocks[r ^ bit] = got[..., k * rows:(k + 1) * rows, :]
    return jnp.concatenate([blocks[r] for r in range(count)], axis=-2)


def dot(a, b, da, db):
    return lax.dot_general(a, b, (((da,), (db,)), ((), ())), preferred_element_type=F32)


TILE = 256
LIGHT = pl.CostEstimate(flops=1, bytes_accessed=1, transcendentals=0)


def cuts(width):
    if width % TILE == 0 and width // TILE >= 4:
        units = width // TILE
        return [(units // 4 + (1 if p < units % 4 else 0)) * TILE for p in range(4)]
    return [width - width // 2, width // 2]


def forward_kernel(count, bit, scaled, grad_out, gate, up, down, *rest):
    keep, send = rest[-2:]
    rows = scaled.shape[0] // count
    for k in range(3):
        if k < 2:
            part = dot(scaled[...], (gate, up)[k][...], 1, 0)
        else:
            part = dot(grad_out[...], down[...], 1, 1)
        kept = sent = 0
        for r in range(count):
            block = part[r * rows:(r + 1) * rows]
            if r & bit:
                send[k, sent * rows:(sent + 1) * rows, :] = block.astype(BF16)
                sent += 1
            else:
                keep[k, kept * rows:(kept + 1) * rows, :] = block
                kept += 1


def forward(scaled, grad_out, gate_weight, up_weight, down_weight, first, size, count, bit, after):
    tokens, local = scaled.shape
    base = first // TILE
    whole = pl.BlockSpec((tokens, local), lambda j: (0, 0))
    column = pl.BlockSpec((local, TILE), lambda j: (0, base + j))
    result = pl.BlockSpec((3, tokens // 2, TILE), lambda j: (0, 0, j))
    extra = list(after)
    return pl.pallas_call(
        functools.partial(forward_kernel, count, bit),
        grid=(size // TILE,),
        in_specs=[whole, whole, column, column, pl.BlockSpec((TILE, local), lambda j: (base + j, 0))]
        + [pl.BlockSpec(memory_space=pl.ANY)] * len(extra),
        out_specs=[result, result],
        out_shape=[
            jax.ShapeDtypeStruct((3, tokens // 2, size), F32),
            jax.ShapeDtypeStruct((3, tokens // 2, size), BF16),
        ],
        compiler_params=pltpu.CompilerParams(vmem_limit_bytes=51 * 2**20),
        cost_estimate=LIGHT,
    )(scaled, grad_out, gate_weight, up_weight, down_weight, *extra)


def activation_kernel(mine, received, inverse, *rest):
    out = rest[-1]
    scale = inverse[...]
    gate = scale * (mine[0] + received[0].astype(F32))
    up_val = scale * (mine[1] + received[1].astype(F32))
    act_grad = mine[2] + received[2].astype(F32)
    sigma = 1.0 / (1.0 + jnp.exp(-gate))
    out[0] = (gate * sigma * up_val).astype(BF16)
    out[1] = (scale * act_grad * up_val * sigma * (1.0 + gate * (1.0 - sigma))).astype(BF16)
    out[2] = (scale * act_grad * gate * sigma).astype(BF16)


def activate(mine, received, inverse, after):
    _, rows, size = mine.shape
    block = pl.BlockSpec((3, rows, TILE), lambda j: (0, 0, j))
    extra = [] if after is None else [after]
    return pl.pallas_call(
        activation_kernel,
        grid=(size // TILE,),
        in_specs=[block, block, pl.BlockSpec((rows, 1), lambda j: (0, 0))]
        + [pl.BlockSpec(memory_space=pl.ANY)] * len(extra),
        out_specs=block,
        out_shape=jax.ShapeDtypeStruct(mine.shape, BF16),
        cost_estimate=LIGHT,
    )(mine, received, inverse, *extra)


def transpose_kernel(x, after, out):
    out[...] = x[...].T


def transpose(x, after):
    rows, columns = x.shape
    return pl.pallas_call(
        transpose_kernel,
        grid=(columns // TILE,),
        in_specs=[pl.BlockSpec((rows, TILE), lambda j: (0, j)), pl.BlockSpec(memory_space=pl.ANY)],
        out_specs=pl.BlockSpec((TILE, rows), lambda j: (j, 0)),
        out_shape=jax.ShapeDtypeStruct((columns, rows), x.dtype),
        cost_estimate=LIGHT,
    )(x, after)


def rows_kernel(mine, received, hidden, gain, after, total, products, gain_part):
    value = mine[...] + received[...].astype(F32)
    term = hidden[...].astype(F32) * value
    total[...] = value
    products[...] = jnp.sum(term * gain[...], axis=1, keepdims=True)
    gain_part[...] = jnp.sum(term, axis=0, keepdims=True)


def finish_rows(mine, received, hidden, gain, after):
    rows, columns = mine.shape
    vmem = pl.BlockSpec(memory_space=pltpu.VMEM)
    return pl.pallas_call(
        rows_kernel,
        in_specs=[vmem] * 4 + [pl.BlockSpec(memory_space=pl.ANY)],
        out_specs=[vmem] * 3,
        out_shape=[
            jax.ShapeDtypeStruct((rows, columns), F32),
            jax.ShapeDtypeStruct((rows, 1), F32),
            jax.ShapeDtypeStruct((1, columns), F32),
        ],
        cost_estimate=LIGHT,
    )(mine, received, hidden, gain[None, :], after)


def grad_rows_kernel(value, hidden, factor, gain, after, out):
    out[...] = (gain[...] * value[...] - hidden[...].astype(F32) * factor[...]).astype(BF16)


def grad_rows(value, hidden, factor, gain, after):
    vmem = pl.BlockSpec(memory_space=pltpu.VMEM)
    return pl.pallas_call(
        grad_rows_kernel,
        in_specs=[vmem] * 4 + [pl.BlockSpec(memory_space=pl.ANY)],
        out_specs=vmem,
        out_shape=jax.ShapeDtypeStruct(value.shape, BF16),
        cost_estimate=LIGHT,
    )(value, hidden, factor[:, None], gain[None, :], after)


def input_step(full, gate, up, before, total):
    @pl.when(pl.program_id(0) == 0)
    def _():
        total[...] = jnp.zeros_like(total) if before is None else before[...]

    total[...] += dot(full[1], gate[...], 1, 1) + dot(full[2], up[...], 1, 1)


def weight_step(full, scaled_t, grad_out, grad_gate, grad_up, grad_down):
    grad_gate[...] = dot(scaled_t[...], full[1], 1, 0).astype(BF16)
    grad_up[...] = dot(scaled_t[...], full[2], 1, 0).astype(BF16)
    grad_down[...] = dot(full[0], grad_out[...], 0, 0).astype(BF16)


def backward_kernel(with_input, with_weights, has_before, has_grads, *refs):
    refs = list(refs)
    full = refs.pop(0)
    if with_input:
        gate, up = refs.pop(0), refs.pop(0)
        before = refs.pop(0) if has_before else None
    if with_weights:
        scaled_t, grad_out = refs.pop(0), refs.pop(0)
        if has_grads:
            refs = refs[3:]
    if with_input:
        input_step(full, gate, up, before, refs.pop(0))
    if with_weights:
        weight_step(full, scaled_t, grad_out, *refs)


def backward(full, first, weights=None, before=None, tall=None, grads=None, shapes=None):
    size = full.shape[2]
    tokens = full.shape[1]
    base = first // TILE
    local = weights[0].shape[0] if weights is not None else tall[0].shape[0]
    column = pl.BlockSpec((local, TILE), lambda j: (0, base + j))
    row = pl.BlockSpec((TILE, local), lambda j: (base + j, 0))
    whole = pl.BlockSpec((tokens, local), lambda j: (0, 0))
    operands = [full]
    in_specs = [pl.BlockSpec((3, tokens, TILE), lambda j: (0, 0, j))]
    out_specs, out_shape, aliases = [], [], {}
    flops = moved = 0
    if weights is not None:
        operands += list(weights)
        in_specs += [column, column]
        if before is not None:
            operands.append(before)
            in_specs.append(whole)
        out_specs.append(whole)
        out_shape.append(jax.ShapeDtypeStruct((tokens, local), F32))
        flops += 4 * tokens * local * size
        moved += 4 * local * size
    if tall is not None:
        operands += list(tall)
        in_specs += [pl.BlockSpec((local, tokens), lambda j: (0, 0)), whole]
        if grads is not None:
            for k in range(3):
                aliases[len(operands) + k] = len(out_shape) + k
            operands += list(grads)
            in_specs += [pl.BlockSpec(memory_space=pl.ANY)] * 3
        out_specs += [column, column, row]
        out_shape += shapes
        flops += 6 * tokens * local * size
        moved += 6 * local * size
    return pl.pallas_call(
        functools.partial(
            backward_kernel, weights is not None, tall is not None, before is not None, grads is not None
        ),
        grid=(size // TILE,),
        in_specs=in_specs,
        out_specs=out_specs,
        out_shape=out_shape,
        input_output_aliases=aliases,
        compiler_params=pltpu.CompilerParams(vmem_limit_bytes=51 * 2**20),
        cost_estimate=LIGHT if weights is not None else pl.CostEstimate(
            flops=flops, bytes_accessed=moved, transcendentals=0
        ),
    )(*operands)


def build(mp, ffn):
    def body(hidden_in, norm_gain, grad_out, gate_weight, up_weight, down_weight):
        tokens, local = hidden_in.shape
        features = local * mp
        width = gate_weight.shape[1]
        m = lax.axis_index("mp")
        f = lax.axis_index("ffn")
        sizes = cuts(width)
        tiled = all(size % TILE == 0 for size in sizes)
        hidden_r = relative(hidden_in, m, mp)
        grad_out_r = relative(grad_out, m, mp)
        scaled = (hidden_r.astype(F32) * norm_gain).astype(BF16)

        hidden = hidden_in.astype(F32)
        square_sum = jnp.sum(hidden * hidden, axis=1)
        order = bits_of(mp)
        square_sums = []
        for bit in order:
            square_sum = square_sum + swap(square_sum, "mp", mp, bit)
            square_sums.append(square_sum)
        inverse = lax.rsqrt(square_sum / features + epsilon)
        mp_rows = tokens // mp
        mine_inverse = lax.dynamic_slice_in_dim(inverse, m * mp_rows, mp_rows, 0)[:, None]
        blocks = list(range(mp))
        first = 0
        starts, kept, sent, arrived = [], [], [], []
        for piece, size in enumerate(sizes):
            way = order if piece % 2 == 0 else order[::-1]
            cols = slice(first, first + size)
            starts.append(first)
            if tiled:
                early = []
                if piece == 0:
                    early = [square_sums[0][None, :]]
                elif piece == 1:
                    early = [mine_inverse]
                elif piece == 2:
                    scaled_t = transpose(scaled, sent[1])
                    early = [scaled_t]
                keep, send = forward(
                    scaled, grad_out_r, gate_weight, up_weight, down_weight, first, size, mp, way[0],
                    sent[-1:] + arrived[:-1][-1:] + early,
                )
            else:
                parts = jnp.stack([
                    dot(scaled, gate_weight[:, cols], 1, 0),
                    dot(scaled, up_weight[:, cols], 1, 0),
                    dot(grad_out_r, down_weight[cols, :], 1, 1),
                ])
                keep = pick(parts, blocks, [r for r in blocks if not r & way[0]], tokens)
                send = pick(parts, blocks, [r for r in blocks if r & way[0]], tokens).astype(BF16)
            kept.append(keep)
            sent.append(send)
            arrived.append(swap(send, "mp", mp, way[0]))
            first += size

        shapes = [
            jax.ShapeDtypeStruct(w.shape, BF16) for w in (gate_weight, up_weight, down_weight)
        ]
        input_part = grads = None
        finals, totals = [], []
        for piece, size in enumerate(sizes):
            way = order if piece % 2 == 0 else order[::-1]
            mine, received = finish_sum(
                kept[piece], arrived[piece], [r for r in blocks if not r & way[0]],
                "mp", mp, way, [BF16] * len(way),
            )
            if tiled:
                results = activate(mine, received, mine_inverse, totals[0] if piece + 1 == len(sizes) else None)
            else:
                sums = mine + received.astype(F32)
                gate = mine_inverse * sums[0]
                up_val = mine_inverse * sums[1]
                act_grad = sums[2]
                sigma = jax.nn.sigmoid(gate)
                activation = (gate * sigma * up_val).astype(BF16)
                gate_grad = (
                    mine_inverse * act_grad * up_val * sigma * (1.0 + gate * (1.0 - sigma))
                ).astype(BF16)
                up_grad = (mine_inverse * act_grad * gate * sigma).astype(BF16)
                results = jnp.stack([activation, gate_grad, up_grad])
            full = gather(results, "mp", mp, way[::-1])
            finals.append(full)
            begin = starts[piece]
            cols = slice(begin, begin + size)
            if not tiled:
                term = dot(full[1], gate_weight[:, cols], 1, 1) + dot(full[2], up_weight[:, cols], 1, 1)
                input_part = term if input_part is None else input_part + term
            elif piece + 1 < len(sizes):
                input_part, *grads = backward(
                    full, begin, (gate_weight, up_weight), input_part, (scaled_t, grad_out_r), grads, shapes
                )
                totals.append(grads[0])
            else:
                input_part, = backward(full, begin, (gate_weight, up_weight), input_part)
                grads = backward(
                    full, begin, tall=(scaled_t, grad_out_r), grads=grads, shapes=shapes
                )

        if not tiled:
            activation, gate_grad, up_grad = (
                jnp.concatenate([full[k] for full in finals], axis=1) for k in range(3)
            )
            grads = [
                dot(scaled, gate_grad, 0, 0).astype(BF16),
                dot(scaled, up_grad, 0, 0).astype(BF16),
                dot(activation, grad_out_r, 0, 0).astype(BF16),
            ]
        grad_gate, grad_up, grad_down = grads
        ffn_order = bits_of(ffn)
        ordered = relative(relative(input_part, m, mp), f, ffn)
        places = list(range(ffn))
        kinds = [F32] + [BF16] * (len(ffn_order) - 1)
        mine = pick(ordered, places, [r for r in places if not r & ffn_order[0]], tokens)
        away = pick(ordered, places, [r for r in places if r & ffn_order[0]], tokens)
        mine, received = scatter_sum(mine, away.astype(kinds[0]), "ffn", ffn, ffn_order, kinds)
        row_count = tokens // ffn
        rows_in = lax.dynamic_slice_in_dim(hidden_in, f * row_count, row_count, 0)
        rows_hidden = rows_in.astype(F32)
        if tiled:
            input_grad, product_part, gain_part = finish_rows(mine, received, rows_in, norm_gain, grads[0])
            product_part, gain_part = product_part[:, 0], gain_part[0]
        else:
            input_grad = mine + received.astype(F32)
            product_part = jnp.sum(norm_gain * rows_hidden * input_grad, axis=1)
            gain_part = jnp.sum(rows_hidden * input_grad, axis=0)
        rows_inverse = lax.dynamic_slice_in_dim(inverse, f * row_count, row_count, 0)
        products = all_sum(product_part, "mp", mp)
        factor = rows_inverse * rows_inverse * products / features
        grad_gain = gain_part
        for bit in ffn_order[:-1]:
            grad_gain = grad_gain + swap(grad_gain, "ffn", ffn, bit)
        if tiled:
            rows_out = grad_rows(input_grad, rows_in, factor, norm_gain, grad_gain[None, :])
        else:
            rows_out = (norm_gain * input_grad - rows_hidden * factor[:, None]).astype(BF16)
        grad_gain = grad_gain + swap(grad_gain, "ffn", ffn, ffn_order[-1])
        grad_hidden = relative(gather(rows_out, "ffn", ffn, ffn_order[::-1]), f, ffn)
        return (grad_hidden, grad_gain, grad_gate, grad_up, grad_down)

    return body


def solution(mesh):
    placed = (P(None, "mp"), P("mp"), P(None, "mp"), P("mp", "ffn"), P("mp", "ffn"), P("ffn", "mp"))
    return jax.shard_map(
        build(mesh.shape["mp"], mesh.shape["ffn"]),
        mesh=mesh,
        in_specs=placed,
        out_specs=(P(None, "mp"), P("mp"), P("mp", "ffn"), P("mp", "ffn"), P("ffn", "mp")),
        check_vma=False,
    )
```
